32 devices in a mesh: pipe: 4 (over z), tensor: 2 (over y), dp: 4 (over x, core).
Axes of the slice: x: 2, y: 2, z: 4, core: 2. Of those that a mesh axis runs over, the one named last changes fastest.
Arguments:
- tokens: bfloat16 [4, 256, 4096], P('pipe', ('tensor', 'dp')), may hold values from -6 to 6
- grad_out: bfloat16 [4, 256, 4096], P('pipe', ('tensor', 'dp')), may hold values from -6 to 6
- weights_in: bfloat16 [4, 2, 14336, 4096], P('pipe', None, ('tensor', 'dp')), may hold values from -0.09375 to 0.09375
- weights_down: bfloat16 [4, 14336, 4096], P('pipe', ('tensor', 'dp')), may hold values from -0.046875 to 0.046875
- projector: bfloat16 [4, 4096, 512], P('pipe'), may hold values from -0.25 to 0.25
- moment_first: float32 [4, 14336, 512], P('pipe', ('tensor', 'dp')), may hold values from -60 to 60
- moment_second: float32 [4, 14336, 512], P('pipe', ('tensor', 'dp')), may hold values from 1 to 10
Outputs:
- grad_prev: bfloat16 [4, 256, 4096], P('pipe', ('tensor', 'dp'))
- update: bfloat16 [4, 14336, 4096], P('pipe', ('tensor', 'dp'))
The draws below stay inside these ranges and needn't reach their ends.
All inputs are finite; a program needn't handle non-finite values.
Results may differ from the reference program's by a relative error of at most 0.0064.
Values may be sent and summed in bfloat16 or wider, within the bound.
No kernel may reach another device: no remote copies, remote signals or barrier semaphores. Data moves between devices by JAX's collectives and lax.ppermute only.
A program may use at most 128 MiB of HBM per device.

```python
import math
import jax
import jax.numpy as jnp

D = 4096
FF = 14336
RANK = 512
TOKENS = 256
N_PIPE = 4


def level_of(rng, shape, pieces, smallest, largest):
    level = 1.0
    for dim, shards_of in pieces:
        steps = jax.random.uniform(jax.random.fold_in(jax.random.fold_in(rng, 6), dim), (shards_of,), jnp.float32, smallest / len(pieces), largest / len(pieces))
        level = level * jnp.repeat(jnp.exp(steps), shape[dim] // shards_of).reshape((-1,) + (1,) * (len(shape) - 1 - dim))
    return level


def bell_draw(key, shape, width, limit, cuts=(), dtype=jnp.bfloat16):
    loudness = level_of(key, shape, cuts, -0.22, 0.18) if cuts else 1.0
    entries = jax.random.normal(key, shape, jnp.float32) * width * loudness
    return jnp.minimum(jnp.maximum(entries, -limit), limit).astype(dtype)


def setup_inputs(seed: int = 0) -> dict:
    keys = jax.random.split(jax.random.key(seed), 8)
    tokens = bell_draw(keys[0], (N_PIPE, TOKENS, D), 1.0, 6.0, ((0, 4), (1, 8)))
    grad_out = bell_draw(keys[1], (N_PIPE, TOKENS, D), 1.0, 6.0, ((0, 4), (1, 8)))
    weights_in = bell_draw(keys[2], (N_PIPE, 2, FF, D), D ** -0.5, 0.09375, ((0, 4), (2, 8)))
    weights_down = bell_draw(keys[3], (N_PIPE, FF, D), FF ** -0.5, 0.046875, ((0, 4), (1, 8)))
    projector = bell_draw(keys[4], (N_PIPE, D, RANK), RANK ** -0.5, 0.25, ((0, 4),))
    moment_first = bell_draw(keys[5], (N_PIPE, FF, RANK), 10.0, 60.0, ((0, 4), (1, 8)), jnp.float32)
    moment_second = jnp.clip(jnp.exp(math.log(10.0) - 2.3025851 * jax.random.uniform(keys[6], (N_PIPE, FF, RANK), jnp.float32) ** level_of(keys[6], (N_PIPE, FF, RANK), ((0, 4), (1, 8)), -0.2, 0.2)), 1.0, 10.0)
    return dict(tokens=tokens, grad_out=grad_out, weights_in=weights_in, weights_down=weights_down, projector=projector, moment_first=moment_first, moment_second=moment_second)


beta_one = 0.9
beta_two = 0.999
bias_one = 1.0 - 0.9 ** 10
bias_two = 1.0 - 0.999 ** 10
epsilon = 1e-08

def adam_update(low_grad, moment_first, moment_second, projector):
    first_moment = beta_one * moment_first + (1.0 - beta_one) * low_grad
    second_moment = beta_two * moment_second + (1.0 - beta_two) * low_grad * low_grad
    normed = (first_moment / bias_one / (jnp.sqrt(second_moment / bias_two) + epsilon)).astype(jnp.bfloat16)
    return jnp.dot(normed, projector.T, preferred_element_type=jnp.float32).astype(jnp.bfloat16)

def section_backward(tokens, grad_out, weights_in, weights_down, projector, moment_first, moment_second):
    gate_pre = jnp.dot(weights_in[0], tokens.T, preferred_element_type=jnp.float32)
    up_act = jnp.dot(weights_in[1], tokens.T, preferred_element_type=jnp.float32)
    sigmoid_gate = jax.nn.sigmoid(gate_pre)
    silu_gate = gate_pre * sigmoid_gate
    hidden = (silu_gate * up_act).astype(jnp.bfloat16)
    grad_hidden = jnp.dot(weights_down, grad_out.T, preferred_element_type=jnp.float32)
    grad_gate = (grad_hidden * up_act * sigmoid_gate * (1.0 + gate_pre * (1.0 - sigmoid_gate))).astype(jnp.bfloat16)
    grad_up = (grad_hidden * silu_gate).astype(jnp.bfloat16)
    grad_in = jnp.dot(grad_gate.T, weights_in[0], preferred_element_type=jnp.float32)
    grad_in = grad_in + jnp.dot(grad_up.T, weights_in[1], preferred_element_type=jnp.float32)
    grad_proj = jnp.dot(grad_out, projector, preferred_element_type=jnp.float32).astype(jnp.bfloat16)
    low_grad = jnp.dot(hidden, grad_proj, preferred_element_type=jnp.float32)
    update = adam_update(low_grad, moment_first, moment_second, projector)
    return (grad_in, update)

def reference(tokens, grad_out, weights_in, weights_down, projector, moment_first, moment_second):
    input_grads = []
    updates = []
    for layer_index in range(N_PIPE):
        grad_in, update = section_backward(tokens[layer_index], grad_out[layer_index], weights_in[layer_index], weights_down[layer_index], projector[layer_index], moment_first[layer_index], moment_second[layer_index])
        input_grads.append(grad_in)
        updates.append(update)
    grad_prev = jnp.roll(jnp.stack(input_grads), -1, axis=0).astype(jnp.bfloat16)
    return (grad_prev, jnp.stack(updates))
```

```python
import functools

import jax
import jax.numpy as jnp
from jax import lax
from jax.experimental import pallas as pl
from jax.experimental.pallas import tpu as pltpu
from jax.sharding import PartitionSpec as P

beta_one = 0.9
beta_two = 0.999
bias_one = 1.0 - 0.9**10
bias_two = 1.0 - 0.999**10
epsilon = 1e-08

BF16 = jnp.bfloat16
F32 = jnp.float32
LANES = 128
VMEM_BYTES = 44 * 2**20
GROUP = ("tensor", "dp")


def dot_nn(a, b):
    return jnp.dot(a, b, preferred_element_type=F32)


def dot_nt(a, b):
    return lax.dot_general(a, b, (((1,), (1,)), ((), ())), preferred_element_type=F32)


def block_of(extent, largest):
    sizes = [size for size in range(LANES, largest + 1, LANES) if extent % size == 0]
    return max(sizes, default=extent)


def whole(shape):
    return pl.BlockSpec(shape, lambda *_: (0,) * len(shape), pipeline_mode=pl.Buffered(1))


def params():
    return pltpu.CompilerParams(vmem_limit_bytes=VMEM_BYTES)


def cost(flops, *arrays):
    moved = sum(a.size * a.dtype.itemsize for a in arrays)
    return pl.CostEstimate(flops=flops, bytes_accessed=moved, transcendentals=0)


def fill(pieces, rows_ref):
    @pl.when(pl.program_id(0) == 0)
    def _():
        start = 0
        for piece in pieces:
            rows_ref[start : start + piece.shape[0], :] = piece[...]
            start += piece.shape[0]


def act_kernel(count, *refs):
    pieces, w_ref = refs[:count], refs[count]
    hidden_ref, gate_ref, up_ref, rows_ref = refs[count + 1 :]
    fill(pieces, rows_ref)
    _, _, block, depth = w_ref.shape
    pre = dot_nt(rows_ref[...], w_ref[0].reshape(2 * block, depth))
    gate_pre, up_act = pre[:, :block], pre[:, block:]
    sigmoid = 1.0 / (1.0 + jnp.exp(-gate_pre))
    silu = gate_pre * sigmoid
    hidden_ref[...] = (silu * up_act).T.astype(BF16)
    gate_ref[...] = up_act * sigmoid * (1.0 + gate_pre * (1.0 - sigmoid))
    up_ref[...] = silu


def activations(pieces, w_in):
    rows = sum(p.shape[0] for p in pieces)
    _, _, units, depth = w_in.shape
    block = block_of(units, 256)
    out_shape = [
        jax.ShapeDtypeStruct((units, rows), BF16),
        jax.ShapeDtypeStruct((rows, units), F32),
        jax.ShapeDtypeStruct((rows, units), F32),
    ]
    return pl.pallas_call(
        functools.partial(act_kernel, len(pieces)),
        name="activations",
        grid=(units // block,),
        in_specs=[whole(p.shape) for p in pieces]
        + [pl.BlockSpec((1, 2, block, depth), lambda i: (0, 0, i, 0))],
        out_specs=[
            pl.BlockSpec((block, rows), lambda i: (i, 0)),
            pl.BlockSpec((rows, block), lambda i: (0, i)),
            pl.BlockSpec((rows, block), lambda i: (0, i)),
        ],
        out_shape=out_shape,
        scratch_shapes=[pltpu.VMEM((rows, depth), BF16)],
        compiler_params=params(),
        cost_estimate=cost(4 * rows * units * depth, w_in, *out_shape),
    )(*pieces, w_in)


def hidden_grad_kernel(count, blocks, *refs):
    pieces, w_ref, gate_ref, up_ref, out_ref, rows_ref = refs[:count], *refs[count:]
    fill(pieces, rows_ref)
    _, block, _ = w_ref.shape
    units = out_ref.shape[1] // 2
    grad = dot_nt(rows_ref[...], w_ref[0])
    if blocks == 1:
        first, second = pl.ds(0, block), pl.ds(units, block)
    else:
        at = pl.program_id(0) * block
        first = pl.ds(pl.multiple_of(at, LANES), block)
        second = pl.ds(pl.multiple_of(at + units, LANES), block)
    out_ref[:, first] = (grad * gate_ref[...]).astype(BF16)
    out_ref[:, second] = (grad * up_ref[...]).astype(BF16)


def hidden_grads(pieces, w_down, gate_factor, up_factor):
    rows = sum(p.shape[0] for p in pieces)
    _, units, depth = w_down.shape
    block = block_of(units, 256)
    blocks = units // block
    out_shape = jax.ShapeDtypeStruct((rows, 2 * units), BF16)
    factor = pl.BlockSpec((rows, block), lambda i: (0, i))
    return pl.pallas_call(
        functools.partial(hidden_grad_kernel, len(pieces), blocks),
        name="hidden_grads",
        grid=(blocks,),
        in_specs=[whole(p.shape) for p in pieces]
        + [pl.BlockSpec((1, block, depth), lambda i: (0, i, 0)), factor, factor],
        out_specs=whole(out_shape.shape),
        out_shape=out_shape,
        scratch_shapes=[pltpu.VMEM((rows, depth), BF16)],
        compiler_params=params(),
        cost_estimate=cost(2 * rows * units * depth, w_down, gate_factor, up_factor, out_shape),
    )(*pieces, w_down, gate_factor, up_factor)


def input_grad_kernel(grads_ref, w_ref, *out_refs):
    _, pair, units, columns = w_ref.shape
    total = dot_nn(grads_ref[...], w_ref[0].reshape(pair * units, columns))
    start = 0
    for out_ref in out_refs:
        out_ref[...] = total[start : start + out_ref.shape[0]].astype(out_ref.dtype)
        start += out_ref.shape[0]


def input_grads(grads, w_in, start, columns, parts):
    rows = grads.shape[0]
    _, _, units, _ = w_in.shape
    block = block_of(columns, 512)
    first = start // block
    out_shape = [jax.ShapeDtypeStruct((count, columns), dtype) for count, dtype in parts]
    return pl.pallas_call(
        input_grad_kernel,
        name="input_grads",
        grid=(columns // block,),
        in_specs=[
            whole(grads.shape),
            pl.BlockSpec((1, 2, units, block), lambda i: (0, 0, 0, first + i)),
        ],
        out_specs=[pl.BlockSpec((count, block), lambda i: (0, i)) for count, _ in parts],
        out_shape=out_shape,
        compiler_params=params(),
        cost_estimate=pl.CostEstimate(
            flops=4 * rows * units * columns,
            bytes_accessed=4 * units * columns + 4 * rows * units + 4 * rows * columns,
            transcendentals=0,
        ),
    )(grads, w_in)


def project_kernel(count, *refs):
    pieces, proj_ref, out_ref, rows_ref = refs[:count], *refs[count:]
    fill(pieces, rows_ref)
    out_ref[...] = dot_nn(rows_ref[...], proj_ref[0]).astype(BF16)


def projected(pieces, projector):
    rows = sum(p.shape[0] for p in pieces)
    _, depth, rank = projector.shape
    out_shape = jax.ShapeDtypeStruct((rows, rank), BF16)
    return pl.pallas_call(
        functools.partial(project_kernel, len(pieces)),
        name="projected",
        grid=(1,),
        in_specs=[whole(p.shape) for p in pieces] + [whole(projector.shape)],
        out_specs=whole(out_shape.shape),
        out_shape=out_shape,
        scratch_shapes=[pltpu.VMEM((rows, depth), BF16)],
        compiler_params=params(),
        cost_estimate=cost(2 * rows * depth * rank, projector, out_shape),
    )(*pieces, projector)


def adam_kernel(hidden_ref, grad_proj_ref, proj_ref, first_ref, second_ref, out_ref):
    low_grad = dot_nn(hidden_ref[...], grad_proj_ref[...])
    first = beta_one * first_ref[0] + (1.0 - beta_one) * low_grad
    second = beta_two * second_ref[0] + (1.0 - beta_two) * low_grad * low_grad
    normed = (first / bias_one / (jnp.sqrt(second / bias_two) + epsilon)).astype(BF16)
    out_ref[0] = dot_nt(normed, proj_ref[0]).astype(BF16)


def adam_update(hidden, grad_proj, projector, moment_first, moment_second):
    units, rows = hidden.shape
    _, depth, rank = projector.shape
    block = block_of(units, 256)
    moment = pl.BlockSpec((1, block, rank), lambda i: (0, i, 0))
    out_shape = jax.ShapeDtypeStruct((1, units, depth), BF16)
    return pl.pallas_call(
        adam_kernel,
        name="adam_update",
        grid=(units // block,),
        in_specs=[
            pl.BlockSpec((block, rows), lambda i: (i, 0)),
            whole(grad_proj.shape),
            whole(projector.shape),
            moment,
            moment,
        ],
        out_specs=pl.BlockSpec((1, block, depth), lambda i: (0, i, 0)),
        out_shape=out_shape,
        compiler_params=params(),
        cost_estimate=cost(
            2 * units * rank * (rows + depth), projector, moment_first, moment_second, out_shape
        ),
    )(hidden, grad_proj, projector, moment_first, moment_second)


class Exchange:
    def __init__(self, mesh):
        self.tensor, self.dp = mesh.shape["tensor"], mesh.shape["dp"]
        self.paired = self.tensor == 2 and self.dp == 4

    def swap(self, value, partner):
        pairs = []
        for t in range(self.tensor):
            for d in range(self.dp):
                to_t, to_d = partner(t, d)
                pairs.append((t * self.dp + d, to_t * self.dp + to_d))
        return lax.ppermute(value, GROUP, pairs)

    def inner(self, value):
        return self.swap(value, lambda t, d: (t, d ^ 1))

    def one(self, value):
        return self.swap(value, lambda t, d: (t ^ (d & 1), d ^ (0 if d & 1 else 2)))

    def two(self, value):
        return self.swap(value, lambda t, d: (t ^ (1 - (d & 1)), d ^ (2 if d & 1 else 0)))

    def gather(self, shard):
        if not self.paired:
            return [lax.all_gather(shard, GROUP, axis=0, tiled=True)]
        two = self.two(shard)
        one = self.one(shard)
        both = self.one(two)
        near = [shard, one, two, both]
        return near + [self.inner(piece) for piece in near]

    def parts(self, rows):
        if not self.paired:
            return [(rows, F32)]
        return [(rows // 2, F32), (rows // 2, BF16)]

    def reduce(self, parts):
        if not self.paired:
            total = lax.psum_scatter(parts[0], GROUP, scatter_dimension=0, tiled=True)
            return total.astype(BF16)
        mine, other = parts
        near = mine + self.inner(other).astype(F32)
        rows = near.shape[0] // 4
        own, one, two, both = (near[i * rows : (i + 1) * rows] for i in range(4))
        both = self.one(both.astype(BF16))
        one = self.one(one.astype(BF16))
        two = self.two((two + both.astype(F32)).astype(BF16))
        return (own + one.astype(F32) + two.astype(F32)).astype(BF16)


def shifted(value, axis, steps):
    count = lax.axis_size(axis)
    pairs = [(source, (source + steps) % count) for source in range(count)]
    return lax.ppermute(value, axis, pairs)


def per_device(
    exchange, tokens, grad_out, w_in, w_down, projector, moment_first, moment_second
):
    depth = tokens.shape[2]
    token_rows = exchange.gather(tokens[0])
    grad_rows = exchange.gather(grad_out[0])
    hidden, gate_factor, up_factor = activations(token_rows, w_in)
    grads = hidden_grads(grad_rows, w_down, gate_factor, up_factor)
    half = depth // 2
    passed = []
    for start in (0, half):
        parts = input_grads(grads, w_in, start, half, exchange.parts(grads.shape[0]))
        passed.append(shifted(exchange.reduce(parts), "pipe", -1))
    grad_proj = projected(grad_rows, projector)
    update = adam_update(hidden, grad_proj, projector, moment_first, moment_second)
    return (jnp.concatenate(passed, axis=1)[None], update)


def solution(mesh):
    spec = P("pipe", GROUP, None)
    return jax.shard_map(
        functools.partial(per_device, Exchange(mesh)),
        mesh=mesh,
        in_specs=(spec, spec, P("pipe", None, GROUP, None), spec, P("pipe", None, None), spec, spec),
        out_specs=(spec, spec),
        check_vma=False,
    )
```

```python
import functools

import jax
import jax.numpy as jnp
from jax import lax
from jax.experimental import pallas as pl
from jax.experimental.pallas import tpu as pltpu
from jax.sharding import PartitionSpec as P

beta_one = 0.9
beta_two = 0.999
bias_one = 1.0 - 0.9**10
bias_two = 1.0 - 0.999**10
epsilon = 1e-08

BF16 = jnp.bfloat16
F32 = jnp.float32
LANES = 128
MIB = 2**20
VMEM = pl.BlockSpec(memory_space=pltpu.VMEM)
ANY = pl.BlockSpec(memory_space=pl.ANY)
HBM = pl.BlockSpec(memory_space=pltpu.HBM)
GROUP = ("tensor", "dp")


def dot_nn(a, b):
    return jnp.dot(a, b, preferred_element_type=F32)


def dot_nt(a, b):
    return lax.dot_general(a, b, (((1,), (1,)), ((), ())), preferred_element_type=F32)


def block_of(extent, largest):
    sizes = [size for size in range(LANES, largest + 1, LANES) if extent % size == 0]
    return max(sizes, default=extent)


def params(*scratch_bytes):
    return pltpu.CompilerParams(vmem_limit_bytes=max(6 * MIB, MIB + sum(scratch_bytes)))


def resident(value):
    return pltpu.with_memory_space_constraint(value, pltpu.VMEM)


def in_hbm(value):
    return pltpu.with_memory_space_constraint(value, pltpu.HBM)


def cost(flops, *arrays):
    moved = sum(a.size * a.dtype.itemsize for a in arrays)
    return pl.CostEstimate(flops=flops, bytes_accessed=moved, transcendentals=0)


def fill(pieces, rows_ref):
    row = column = 0
    for piece in pieces:
        rows, columns = piece.shape
        rows_ref[row : row + rows, column : column + columns] = piece[...]
        column += columns
        if column == rows_ref.shape[1]:
            row, column = row + rows, 0


def rows_of(pieces, depth):
    return sum(piece.size for piece in pieces) // depth


MARK = jax.ShapeDtypeStruct((8, LANES), F32)


def after_kernel(*_):
    pass


def after(value, *others):
    return pl.pallas_call(
        after_kernel,
        name="after",
        in_specs=[ANY] * (1 + len(others)),
        out_specs=ANY,
        out_shape=jax.ShapeDtypeStruct(value.shape, value.dtype),
        input_output_aliases={0: 0},
        compiler_params=params(),
        cost_estimate=pl.CostEstimate(flops=0, bytes_accessed=0, transcendentals=0),
    )(value, *others)


def stream(reads, slots):
    for read in reads[:slots]:
        read.start()

    def wait(step):
        reads[step].wait()

    def refill(step):
        if step + slots < len(reads):
            reads[step + slots].start()

    return wait, refill


def load_kernel(units, w_ref, out_ref, mark_ref, sem):
    here = pl.ds(0, units)
    copy = pltpu.make_async_copy(w_ref.at[:, :, here, :], out_ref.at[:, :, here, :], sem)
    copy.start()
    mark_ref[...] = jnp.zeros_like(mark_ref)
    copy.wait()


def load(w_in, units, limit):
    return pl.pallas_call(
        functools.partial(load_kernel, units),
        name="load",
        in_specs=[HBM],
        out_specs=[VMEM, VMEM],
        out_shape=[pltpu.VMEM(w_in.shape, w_in.dtype), MARK],
        scratch_shapes=[pltpu.SemaphoreType.DMA],
        compiler_params=params(limit),
        cost_estimate=cost(0),
    )(in_hbm(w_in))


def act_kernel(count, loaded, *refs):
    pieces, w_ref = refs[:count], refs[count]
    hidden_ref, gate_ref, up_ref, mark_ref, held_ref, rows_ref, sems = refs[count + 2 :]
    _, _, units, depth = held_ref.shape
    block = block_of(units, 256)
    reads = []
    for step, start in enumerate(range(0, units, block)):
        here = pl.ds(start, block)
        if start < loaded:
            reads.append(None)
            continue
        reads.append(
            pltpu.make_async_copy(
                w_ref.at[0, :, here, :], held_ref.at[0, :, here, :], sems.at[step]
            )
        )
        reads[-1].start()
    mark_ref[...] = jnp.zeros_like(mark_ref)
    fill(pieces, rows_ref)

    def finish(step, pre):
        gate_pre, up_act = pre[:, :block], pre[:, block:]
        sigmoid = 1.0 / (1.0 + jnp.exp(-gate_pre))
        silu = gate_pre * sigmoid
        here = slice(step * block, (step + 1) * block)
        hidden_ref[here, :] = (silu * up_act).T.astype(BF16)
        gate_ref[:, here] = up_act * sigmoid * (1.0 + gate_pre * (1.0 - sigmoid))
        up_ref[:, here] = silu

    before = None
    for step, read in enumerate(reads):
        if read is not None:
            read.wait()
        w = held_ref[0, :, step * block : (step + 1) * block, :].reshape(2 * block, depth)
        pre = dot_nt(rows_ref[...], w)
        if before is not None:
            finish(step - 1, before)
        before = pre
    finish(len(reads) - 1, before)


def activations(pieces, w_in, held, loaded, limit):
    _, _, units, depth = w_in.shape
    rows = rows_of(pieces, depth)
    block = block_of(units, 256)
    out_shape = [
        jax.ShapeDtypeStruct((units, rows), BF16),
        jax.ShapeDtypeStruct((rows, units), F32),
        jax.ShapeDtypeStruct((rows, units), F32),
        MARK,
        pltpu.VMEM(w_in.shape, w_in.dtype),
    ]
    return pl.pallas_call(
        functools.partial(act_kernel, len(pieces), loaded),
        name="activations",
        in_specs=[VMEM] * len(pieces) + [HBM, VMEM],
        out_specs=[VMEM] * 5,
        out_shape=out_shape,
        input_output_aliases={len(pieces) + 1: 4},
        scratch_shapes=[
            pltpu.VMEM((rows, depth), BF16),
            pltpu.SemaphoreType.DMA((units // block,)),
        ],
        compiler_params=params(limit),
        cost_estimate=cost(4 * rows * units * depth),
    )(*pieces, in_hbm(w_in), held)


def input_grad_kernel(count, slots, *refs):
    pieces = refs[:count]
    down_ref, w_ref, gate_ref, up_ref = refs[count : count + 4]
    outs = refs[count + 4 : -4]
    rows_ref, grads_ref, slots_ref, sems = refs[-4:]
    _, pair, units, depth = w_ref.shape
    size = slots_ref.shape[1]
    starts = range(0, units, size)
    sizes = [min(size, units - start) for start in starts]
    wait, refill = stream(
        [
            pltpu.make_async_copy(
                down_ref.at[0, pl.ds(start, size), :],
                slots_ref.at[step % slots, pl.ds(0, size), :],
                sems.at[step % slots],
            )
            for step, (start, size) in enumerate(zip(starts, sizes))
        ],
        slots,
    )
    fill(pieces, rows_ref)

    def finish(step, grad):
        here = slice(starts[step], starts[step] + sizes[step])
        there = slice(units + here.start, units + here.stop)
        grads_ref[:, here] = (grad * gate_ref[:, here]).astype(BF16)
        grads_ref[:, there] = (grad * up_ref[:, here]).astype(BF16)

    before = None
    for step, size in enumerate(sizes):
        wait(step)
        grad = dot_nt(rows_ref[...], slots_ref[step % slots, :size, :])
        if before is not None:
            finish(step - 1, before)
        refill(step)
        before = grad
    finish(len(sizes) - 1, before)
    block = block_of(depth, 1024)
    for start in range(0, depth, block):
        here = slice(start, start + block)
        total = dot_nn(grads_ref[...], w_ref[0, :, :, here].reshape(pair * units, block))
        row = 0
        for out_ref in outs:
            rows = out_ref.shape[0]
            out_ref[:, here] = total[row : row + rows].astype(out_ref.dtype)
            row += rows


def down_blocks(units):
    size = block_of(units, 256)
    size = 2 * size if units > size else units
    return size, min(2, -(-units // size))


def vmem_limit(rows, w_in, exchange):
    _, _, units, depth = w_in.shape
    size, slots = down_blocks(units)
    scratch = 2 * rows * depth + 4 * rows * units + 2 * slots * size * depth
    work = 16 * rows * max(size, block_of(depth, 1024))
    return scratch + work + (0 if exchange.paired else 4 * rows * depth)


def input_grads(pieces, w_down, held, gate_factor, up_factor, exchange, limit):
    rows, units = gate_factor.shape
    depth = held.shape[3]
    parts = exchange.parts(rows)
    size, slots = down_blocks(units)
    out_shape = [jax.ShapeDtypeStruct((count, depth), dtype) for count, dtype in parts]
    return pl.pallas_call(
        functools.partial(input_grad_kernel, len(pieces), slots),
        name="input_grads",
        in_specs=[VMEM] * len(pieces) + [HBM] + [VMEM] * 3,
        out_specs=[VMEM] * len(parts),
        out_shape=out_shape,
        scratch_shapes=[
            pltpu.VMEM((rows, depth), BF16),
            pltpu.VMEM((rows, 2 * units), BF16),
            pltpu.VMEM((slots, size, depth), BF16),
            pltpu.SemaphoreType.DMA((slots,)),
        ],
        compiler_params=params(limit),
        cost_estimate=cost(6 * rows * units * depth, w_down, *out_shape),
    )(*pieces, in_hbm(w_down), held, gate_factor, up_factor)


def project_kernel(count, *refs):
    pieces, proj_ref, out_ref, rows_ref = refs[:count], *refs[count:]
    fill(pieces, rows_ref)
    out_ref[...] = dot_nn(rows_ref[...], proj_ref[0]).astype(BF16)


def projected(pieces, projector):
    _, depth, rank = projector.shape
    rows = rows_of(pieces, depth)
    out_shape = jax.ShapeDtypeStruct((rows, rank), BF16)
    return pl.pallas_call(
        functools.partial(project_kernel, len(pieces)),
        name="projected",
        in_specs=[VMEM] * (len(pieces) + 1),
        out_specs=VMEM,
        out_shape=out_shape,
        scratch_shapes=[pltpu.VMEM((rows, depth), BF16)],
        compiler_params=params(2 * rows * depth, 8 * rows * rank),
        cost_estimate=cost(2 * rows * depth * rank, projector),
    )(*pieces, projector)


def adam_kernel(start, block, held, *refs):
    hidden_ref, grad_proj_ref, proj_ref, first_ref, second_ref = refs[:5]
    out_ref, mark_ref, normed_ref, moments_ref, slots_ref, in_sems, out_sems = refs[5 + held :]
    units, depth = normed_ref.shape[0], proj_ref.shape[1]
    width = block_of(depth, 1024)
    steps = range(0, units, block)

    reads = []
    for step, at in enumerate(steps):
        there = pl.ds(start + at, block)
        for which, ref in enumerate((first_ref, second_ref)):
            reads.append(
                pltpu.make_async_copy(
                    ref.at[0, there, :],
                    moments_ref.at[which, pl.ds(at, block), :],
                    in_sems.at[which, step],
                )
            )
    for read in reads:
        read.start()
    mark_ref[...] = jnp.zeros_like(mark_ref)

    def wait(step):
        for read in reads[2 * step : 2 * step + 2]:
            read.wait()

    def normalise(step):
        here = slice(step * block, (step + 1) * block)
        low_grad = dot_nn(
            hidden_ref[start + here.start : start + here.stop, :], grad_proj_ref[...]
        )
        first = beta_one * moments_ref[0, here, :] + (1.0 - beta_one) * low_grad
        second = beta_two * moments_ref[1, here, :] + (1.0 - beta_two) * low_grad * low_grad
        normed = first / bias_one / (jnp.sqrt(second / bias_two) + epsilon)
        normed_ref[here, :] = normed.astype(BF16)

    writes = []
    wait(0)
    normalise(0)
    for step, at in enumerate(steps):
        slot = step % 2
        if step >= 2:
            for write in writes[step - 2]:
                write.wait()
        if step + 1 < len(steps):
            wait(step + 1)
            normalise(step + 1)
        for column in range(0, depth, width):
            here = slice(column, column + width)
            back = dot_nt(normed_ref[at : at + block, :], proj_ref[0, here, :])
            slots_ref[slot, :, here] = back.astype(BF16)
            write = pltpu.make_async_copy(
                slots_ref.at[slot, :, pl.ds(column, width)],
                out_ref.at[0, pl.ds(start + at, block), pl.ds(column, width)],
                out_sems.at[slot, column // width],
            )
            write.start()
            if not column:
                writes.append([])
            writes[-1].append(write)
    for step in writes[-2:]:
        for write in step:
            write.wait()


def adam_update(hidden, grad_proj, projector, moment_first, moment_second, start, units, out=None):
    rows = hidden.shape[1]
    _, all_units, rank = moment_first.shape
    depth = projector.shape[1]
    block = block_of(all_units, 256)
    held = [] if out is None else [out]
    out_shape = jax.ShapeDtypeStruct((1, all_units, depth), BF16)
    return pl.pallas_call(
        functools.partial(adam_kernel, start, block, len(held)),
        name="adam_update",
        in_specs=[VMEM] * 3 + [HBM] * (2 + len(held)),
        out_specs=[HBM, VMEM],
        out_shape=[out_shape, MARK],
        input_output_aliases={5: 0} if held else {},
        scratch_shapes=[
            pltpu.VMEM((units, rank), BF16),
            pltpu.VMEM((2, units, rank), F32),
            pltpu.VMEM((2, block, depth), BF16),
            pltpu.SemaphoreType.DMA((2, units // block)),
            pltpu.SemaphoreType.DMA((2, depth // block_of(depth, 1024))),
        ],
        compiler_params=params(10 * units * rank, 8 * block * depth, 16 * block * rank),
        cost_estimate=pl.CostEstimate(
            flops=2 * units * rank * (rows + depth), bytes_accessed=2 * units * depth, transcendentals=0
        ),
    )(hidden, grad_proj, projector, in_hbm(moment_first), in_hbm(moment_second), *held)


class Exchange:
    def __init__(self, mesh):
        self.tensor, self.dp = mesh.shape["tensor"], mesh.shape["dp"]
        self.paired = self.tensor == 2 and self.dp == 4

    def swap(self, value, partner):
        pairs = []
        for t in range(self.tensor):
            for d in range(self.dp):
                to_t, to_d = partner(t, d)
                pairs.append((t * self.dp + d, to_t * self.dp + to_d))
        return lax.ppermute(value, GROUP, pairs)

    def inner(self, value):
        return self.swap(value, lambda t, d: (t, d ^ 1))

    def one(self, value):
        return self.swap(value, lambda t, d: (t ^ (d & 1), d ^ (0 if d & 1 else 2)))

    def two(self, value):
        return self.swap(value, lambda t, d: (t ^ (1 - (d & 1)), d ^ (2 if d & 1 else 0)))

    def gather(self, shard, wait=lambda value: value):
        if not self.paired:
            return [lax.all_gather(shard, GROUP, axis=0, tiled=True)]
        two, one = self.two(shard), self.one(shard)
        return [shard, one, two, self.one(wait(two))]

    def share(self, near):
        if not self.paired:
            return near
        return near + [self.inner(piece) for piece in near]

    def parts(self, rows):
        if not self.paired:
            return [(rows, F32)]
        return [(rows // 2, F32), (rows // 2, BF16)]

    def reduce(self, parts, meanwhile):
        if not self.paired:
            total = lax.psum_scatter(parts[0], GROUP, scatter_dimension=0, tiled=True)
            return total.astype(BF16)
        mine, other = parts
        near = mine + meanwhile(None, self.inner(other)).astype(F32)
        shard = near.shape[0] // 4
        own, one, two, both = (near[i * shard : (i + 1) * shard] for i in range(4))
        half = own.shape[1] // 2
        both = both.astype(BF16)
        left = meanwhile(both, self.one(both[:, :half]))
        right = self.two(both[:, half:])
        two = jnp.concatenate([two[:, :half] + left.astype(F32), two[:, half:]], axis=1)
        one = jnp.concatenate([one[:, :half], one[:, half:] + right.astype(F32)], axis=1)
        two, one = two.astype(BF16), one.astype(BF16)
        one = meanwhile(one, self.one(one))
        two = self.two(two)
        return (own + one.astype(F32) + two.astype(F32)).astype(BF16)


def shifted(value, axis, steps):
    count = lax.axis_size(axis)
    pairs = [(source, (source + steps) % count) for source in range(count)]
    return lax.ppermute(value, axis, pairs)


def per_device(
    exchange, tokens, grad_out, w_in, w_down, projector, moment_first, moment_second
):
    units = w_in.shape[2]
    block = block_of(units, 256)
    rows = tokens.shape[1] * exchange.tensor * exchange.dp
    limit = vmem_limit(rows, w_in, exchange)
    early = block * (units // block // 2)
    held, loaded = load(w_in, early, limit) if early else load(w_in, units, limit)
    token_rows = exchange.share(exchange.gather(tokens[0], lambda two: after(two, loaded)))
    grad_rows = exchange.gather(grad_out[0])
    hidden, gate_factor, up_factor, mark, held = activations(
        token_rows, w_in, held, early or units, limit
    )
    if len(grad_rows) > 1:
        grad_rows = grad_rows[:3] + [after(piece, mark) for piece in grad_rows[3:]]
    grad_rows = exchange.share(grad_rows)
    parts = input_grads(grad_rows, w_down, held, gate_factor, up_factor, exchange, limit)
    projector = resident(projector)
    grad_proj = projected(grad_rows[:-1] + [after(grad_rows[-1], parts[0])], projector)
    cut = block * -(-units // (3 * block))
    ranges = [(start, min(cut, units - start)) for start in range(0, units, cut)]
    update = None

    def meanwhile(sent, received):
        nonlocal update
        if sent is None:
            return after(received, grad_proj)
        if not ranges:
            return received
        start, count = ranges.pop()
        update, mark = adam_update(
            hidden, after(grad_proj, sent), projector, moment_first, moment_second, start, count, update
        )
        return after(received, mark)

    total = exchange.reduce(parts, meanwhile)
    passed = shifted(total, "pipe", -1)
    for start, count in ranges[::-1]:
        update, _ = adam_update(
            hidden, after(grad_proj, total), projector, moment_first, moment_second, start, count, update
        )
    return (passed[None], update)


def solution(mesh):
    spec = P("pipe", GROUP, None)
    return jax.shard_map(
        functools.partial(per_device, Exchange(mesh)),
        mesh=mesh,
        in_specs=(spec, spec, P("pipe", None, GROUP, None), spec, P("pipe", None, None), spec, spec),
        out_specs=(spec, spec),
        check_vma=False,
    )
```

```python
import functools

import jax
import jax.numpy as jnp
from jax import lax
from jax.experimental import pallas as pl
from jax.experimental.pallas import tpu as pltpu
from jax.sharding import PartitionSpec as P

beta_one = 0.9
beta_two = 0.999
bias_one = 1.0 - 0.9**10
bias_two = 1.0 - 0.999**10
epsilon = 1e-08

BF16 = jnp.bfloat16
F32 = jnp.float32
LANES = 128
MIB = 2**20
VMEM = pl.BlockSpec(memory_space=pltpu.VMEM)
ANY = pl.BlockSpec(memory_space=pl.ANY)
HBM = pl.BlockSpec(memory_space=pltpu.HBM)
GROUP = ("tensor", "dp")


def dot_nn(a, b):
    return jnp.dot(a, b, preferred_element_type=F32)


def dot_nt(a, b):
    return lax.dot_general(a, b, (((1,), (1,)), ((), ())), preferred_element_type=F32)


def block_of(extent, largest):
    sizes = [size for size in range(LANES, largest + 1, LANES) if extent % size == 0]
    return max(sizes, default=extent)


def params(*scratch_bytes):
    return pltpu.CompilerParams(vmem_limit_bytes=max(6 * MIB, MIB + sum(scratch_bytes)))


def resident(value):
    return pltpu.with_memory_space_constraint(value, pltpu.VMEM)


def in_hbm(value):
    return pltpu.with_memory_space_constraint(value, pltpu.HBM)


def cost(flops, *arrays):
    moved = sum(a.size * a.dtype.itemsize for a in arrays)
    return pl.CostEstimate(flops=flops, bytes_accessed=moved, transcendentals=0)


def fill(pieces, rows_ref):
    row = column = 0
    for piece in pieces:
        rows, columns = piece.shape
        rows_ref[row : row + rows, column : column + columns] = piece[...]
        column += columns
        if column == rows_ref.shape[1]:
            row, column = row + rows, 0


def rows_of(pieces, depth):
    return sum(piece.size for piece in pieces) // depth


MARK = jax.ShapeDtypeStruct((8, LANES), F32)


def after_kernel(*_):
    pass


def after(value, *others):
    return pl.pallas_call(
        after_kernel,
        name="after",
        in_specs=[ANY] * (1 + len(others)),
        out_specs=ANY,
        out_shape=jax.ShapeDtypeStruct(value.shape, value.dtype),
        input_output_aliases={0: 0},
        compiler_params=params(),
        cost_estimate=pl.CostEstimate(flops=0, bytes_accessed=0, transcendentals=0),
    )(value, *others)


def stream(reads, slots):
    for read in reads[:slots]:
        read.start()

    def wait(step):
        reads[step].wait()

    def refill(step):
        if step + slots < len(reads):
            reads[step + slots].start()

    return wait, refill


def block_reads(w_ref, held_ref, sems, start, stop):
    units = w_ref.shape[2]
    block = block_of(units, 256)
    return [
        [
            pltpu.make_async_copy(
                w_ref.at[0, which, pl.ds(at, block), :],
                held_ref.at[pl.ds(2 * at + which * block, block), :],
                sems.at[at // block, which],
            )
            for which in range(2)
        ]
        for at in range(start, stop, block)
    ]


def down_early(units):
    block = block_of(units, 256)
    return block * -(-units // (2 * block)) - (block if units > block else 0)


def load_kernel(units, w_ref, held_ref, mark_ref, sems):
    pairs = block_reads(w_ref, held_ref, sems, 0, units)
    for pair in pairs:
        for read in pair:
            read.start()
    mark_ref[...] = jnp.zeros_like(mark_ref)
    for pair in pairs:
        for read in pair:
            read.wait()


def load(w_in, units, limit):
    _, _, all_units, depth = w_in.shape
    return pl.pallas_call(
        functools.partial(load_kernel, units),
        name="load",
        in_specs=[HBM],
        out_specs=[VMEM, VMEM],
        out_shape=[pltpu.VMEM((2 * all_units + down_early(all_units), depth), w_in.dtype), MARK],
        scratch_shapes=[pltpu.SemaphoreType.DMA((units // block_of(all_units, 256), 2))],
        compiler_params=params(limit),
        cost_estimate=cost(0),
    )(in_hbm(w_in))


def act_kernel(count, loaded, *refs):
    pieces, w_ref, down_ref = refs[:count], refs[count], refs[count + 1]
    outs, (rows_ref, sems, down_sem) = refs[count + 3 : -3], refs[-3:]
    hidden_ref, gate_ref, up_ref, mark_ref, held_ref = outs
    _, units, depth = down_ref.shape
    block = block_of(units, 256)
    pairs = block_reads(w_ref, held_ref, sems, loaded, units)
    for pair in pairs:
        for read in pair:
            read.start()
    down_read = pltpu.make_async_copy(
        down_ref.at[0, pl.ds(0, held_ref.shape[0] - 2 * units), :],
        held_ref.at[pl.ds(2 * units, held_ref.shape[0] - 2 * units), :],
        down_sem,
    )
    mark_ref[...] = jnp.zeros_like(mark_ref)
    fill(pieces, rows_ref)

    def finish(at, pre):
        gate_pre, up_act = pre[:, :block], pre[:, block:]
        sigmoid = 1.0 / (1.0 + jnp.exp(-gate_pre))
        silu = gate_pre * sigmoid
        here = slice(at, at + block)
        hidden_ref[here, :] = (silu * up_act).T.astype(BF16)
        gate_ref[:, here] = up_act * sigmoid * (1.0 + gate_pre * (1.0 - sigmoid))
        up_ref[:, here] = silu

    for at in range(0, units, block):
        if at >= loaded:
            for read in pairs[(at - loaded) // block]:
                read.wait()
        pre = dot_nt(rows_ref[...], held_ref[2 * at : 2 * (at + block), :])
        if at == 0:
            down_read.start()
        else:
            finish(at - block, before)
        before = pre
    finish(units - block, before)
    down_read.wait()


def activations(pieces, w_in, w_down, held, loaded, limit):
    _, _, units, depth = w_in.shape
    rows = rows_of(pieces, depth)
    out_shape = [
        jax.ShapeDtypeStruct((units, rows), BF16),
        jax.ShapeDtypeStruct((rows, units), F32),
        jax.ShapeDtypeStruct((rows, units), F32),
        MARK,
        pltpu.VMEM(held.shape, held.dtype),
    ]
    return pl.pallas_call(
        functools.partial(act_kernel, len(pieces), loaded),
        name="activations",
        in_specs=[VMEM] * len(pieces) + [HBM, HBM, VMEM],
        out_specs=[VMEM] * 5,
        out_shape=out_shape,
        input_output_aliases={len(pieces) + 2: 4},
        scratch_shapes=[
            pltpu.VMEM((rows, depth), BF16),
            pltpu.SemaphoreType.DMA((units // block_of(units, 256), 2)),
            pltpu.SemaphoreType.DMA,
        ],
        compiler_params=params(limit),
        cost_estimate=cost(4 * rows * units * depth),
    )(*pieces, in_hbm(w_in), in_hbm(w_down), held)


def input_grad_kernel(count, *refs):
    pieces = refs[:count]
    down_ref, held_ref, gate_ref, up_ref = refs[count : count + 4]
    outs, (rows_ref, grads_ref, slots_ref, sems) = refs[count + 4 : -4], refs[-4:]
    units, depth = gate_ref.shape[1], held_ref.shape[1]
    early = held_ref.shape[0] - 2 * units
    slots, step, _ = slots_ref.shape
    rest = range(early, units, step)
    wait, refill = stream(
        [
            pltpu.make_async_copy(
                down_ref.at[0, pl.ds(start, step), :],
                slots_ref.at[number % slots],
                sems.at[number % slots],
            )
            for number, start in enumerate(rest)
        ],
        slots,
    )
    fill(pieces, rows_ref)

    def factor(start, grad):
        for at in range(start, start + grad.shape[1], step):
            here, part = slice(at, at + step), grad[:, at - start : at - start + step]
            grads_ref[:, 2 * at : 2 * at + step] = (part * gate_ref[:, here]).astype(BF16)
            grads_ref[:, 2 * at + step : 2 * (at + step)] = (part * up_ref[:, here]).astype(BF16)

    wide = min(units, 2 * step)
    for start in range(0, early, wide):
        stop = min(start + wide, early)
        factor(start, dot_nt(rows_ref[...], held_ref[2 * units + start : 2 * units + stop, :]))
    for number, start in enumerate(rest):
        wait(number)
        grad = dot_nt(rows_ref[...], slots_ref[number % slots])
        refill(number)
        factor(start, grad)
    block = block_of(depth, 1024)
    for start in range(0, depth, block):
        here = slice(start, start + block)
        total = dot_nn(grads_ref[...], held_ref[: 2 * units, here])
        row = 0
        for out_ref in outs:
            rows = out_ref.shape[0]
            out_ref[:, here] = total[row : row + rows].astype(out_ref.dtype)
            row += rows


def vmem_limit(rows, w_in, exchange):
    _, _, units, depth = w_in.shape
    work = 8 * rows * max(min(units, 512), block_of(depth, 1024))
    slots = 2 * block_of(units, 256) if units > block_of(units, 256) else 0
    scratch = 2 * rows * depth + 4 * rows * units + 2 * slots * depth
    return scratch + (work if exchange.paired else 3 * work + 4 * rows * depth)


def input_grads(pieces, w_down, held, gate_factor, up_factor, exchange, limit):
    rows, units = gate_factor.shape
    depth = held.shape[1]
    parts = exchange.parts(rows)
    step = block_of(units, 256)
    out_shape = [jax.ShapeDtypeStruct((count, depth), dtype) for count, dtype in parts]
    return pl.pallas_call(
        functools.partial(input_grad_kernel, len(pieces)),
        name="input_grads",
        in_specs=[VMEM] * len(pieces) + [HBM] + [VMEM] * 3,
        out_specs=[VMEM] * len(parts),
        out_shape=out_shape,
        scratch_shapes=[
            pltpu.VMEM((rows, depth), BF16),
            pltpu.VMEM((rows, 2 * units), BF16),
            pltpu.VMEM((2 if units > step else 1, step, depth), BF16),
            pltpu.SemaphoreType.DMA((2 if units > step else 1,)),
        ],
        compiler_params=params(limit),
        cost_estimate=cost(6 * rows * units * depth, *out_shape),
    )(*pieces, in_hbm(w_down), held, gate_factor, up_factor)


def project_kernel(count, *refs):
    pieces = refs[:count]
    proj_ref, first_ref, second_ref, out_ref, moments_ref, rows_ref, sems = refs[count:]
    here = pl.ds(0, moments_ref.shape[1])
    reads = [
        pltpu.make_async_copy(ref.at[0, here, :], moments_ref.at[which], sems.at[which])
        for which, ref in enumerate((first_ref, second_ref))
    ]
    for read in reads:
        read.start()
    fill(pieces, rows_ref)
    out_ref[...] = dot_nn(rows_ref[...], proj_ref[0]).astype(BF16)
    for read in reads:
        read.wait()


def projected(pieces, projector, moment_first, moment_second, units):
    _, depth, rank = projector.shape
    rows = rows_of(pieces, depth)
    out_shape = [
        jax.ShapeDtypeStruct((rows, rank), BF16),
        pltpu.VMEM((2, units, rank), F32),
    ]
    return pl.pallas_call(
        functools.partial(project_kernel, len(pieces)),
        name="projected",
        in_specs=[VMEM] * (len(pieces) + 1) + [HBM] * 2,
        out_specs=[VMEM] * 2,
        out_shape=out_shape,
        scratch_shapes=[pltpu.VMEM((rows, depth), BF16), pltpu.SemaphoreType.DMA((2,))],
        compiler_params=adam_params(depth, rank, rows),
        cost_estimate=cost(2 * rows * depth * rank, projector),
    )(*pieces, projector, in_hbm(moment_first), in_hbm(moment_second))


def adam_params(depth, rank, rows):
    return params(2 * rows * depth, 8 * rows * rank, 20 * 2**20)


def adam_kernel(start, block, held, ready, *refs):
    hidden_ref, grad_proj_ref, proj_ref, ready_ref, first_ref, second_ref = refs[:6]
    out_ref, mark_ref, normed_ref, moments_ref, slots_ref, in_sems, out_sems = refs[6 + held :]
    units, depth = normed_ref.shape[0], proj_ref.shape[1]
    width = block_of(depth, 1024)
    steps = range(0, units, block)

    reads = []
    for step, at in enumerate(() if ready else steps):
        there = pl.ds(start + at, block)
        for which, ref in enumerate((first_ref, second_ref)):
            reads.append(
                pltpu.make_async_copy(
                    ref.at[0, there, :],
                    moments_ref.at[which, pl.ds(at, block), :],
                    in_sems.at[which, step],
                )
            )
    for read in reads:
        read.start()
    mark_ref[...] = jnp.zeros_like(mark_ref)

    def wait(step):
        for read in reads[2 * step : 2 * step + 2]:
            read.wait()

    def moments(which, here):
        if ready:
            return ready_ref[which, start + here.start : start + here.stop, :]
        return moments_ref[which, here, :]

    def normalise(step):
        here = slice(step * block, (step + 1) * block)
        low_grad = dot_nn(
            hidden_ref[start + here.start : start + here.stop, :], grad_proj_ref[...]
        )
        first = beta_one * moments(0, here) + (1.0 - beta_one) * low_grad
        second = beta_two * moments(1, here) + (1.0 - beta_two) * low_grad * low_grad
        normed = first / bias_one / (jnp.sqrt(second / bias_two) + epsilon)
        normed_ref[here, :] = normed.astype(BF16)

    writes = []
    wait(0)
    normalise(0)
    for step, at in enumerate(steps):
        slot = step % 2
        if step >= 2:
            for write in writes[step - 2]:
                write.wait()
        if step + 1 < len(steps):
            wait(step + 1)
            normalise(step + 1)
        for column in range(0, depth, width):
            here = slice(column, column + width)
            back = dot_nt(normed_ref[at : at + block, :], proj_ref[0, here, :])
            slots_ref[slot, :, here] = back.astype(BF16)
            write = pltpu.make_async_copy(
                slots_ref.at[slot, :, pl.ds(column, width)],
                out_ref.at[0, pl.ds(start + at, block), pl.ds(column, width)],
                out_sems.at[slot, column // width],
            )
            write.start()
            if not column:
                writes.append([])
            writes[-1].append(write)
    for step in writes[-2:]:
        for write in step:
            write.wait()


def adam_update(hidden, grad_proj, projector, ready, moments, start, units, out=None):
    rows = hidden.shape[1]
    _, all_units, rank = moments[0].shape
    depth = projector.shape[1]
    block = block_of(all_units, 256)
    held = [] if out is None else [out]
    early = start + units <= ready.shape[1]
    out_shape = jax.ShapeDtypeStruct((1, all_units, depth), BF16)
    return pl.pallas_call(
        functools.partial(adam_kernel, start, block, len(held), early),
        name="adam_update",
        in_specs=[VMEM] * 4 + [HBM] * (2 + len(held)),
        out_specs=[HBM, VMEM],
        out_shape=[out_shape, MARK],
        input_output_aliases={6: 0} if held else {},
        scratch_shapes=[
            pltpu.VMEM((units, rank), BF16),
            pltpu.VMEM((2, block if early else units, rank), F32),
            pltpu.VMEM((2, block, depth), BF16),
            pltpu.SemaphoreType.DMA((2, units // block)),
            pltpu.SemaphoreType.DMA((2, depth // block_of(depth, 1024))),
        ],
        compiler_params=adam_params(depth, rank, rows),
        cost_estimate=pl.CostEstimate(
            flops=2 * units * rank * (rows + depth), bytes_accessed=2 * units * depth, transcendentals=0
        ),
    )(hidden, grad_proj, projector, ready, *map(in_hbm, moments), *held)


class Exchange:
    def __init__(self, mesh):
        self.tensor, self.dp = mesh.shape["tensor"], mesh.shape["dp"]
        self.paired = self.tensor == 2 and self.dp == 4

    def swap(self, value, partner):
        pairs = []
        for t in range(self.tensor):
            for d in range(self.dp):
                to_t, to_d = partner(t, d)
                pairs.append((t * self.dp + d, to_t * self.dp + to_d))
        return lax.ppermute(value, GROUP, pairs)

    def inner(self, value):
        return self.swap(value, lambda t, d: (t, d ^ 1))

    def one(self, value):
        return self.swap(value, lambda t, d: (t ^ (d & 1), d ^ (0 if d & 1 else 2)))

    def two(self, value):
        return self.swap(value, lambda t, d: (t ^ (1 - (d & 1)), d ^ (2 if d & 1 else 0)))

    def gather(self, shard, wait=lambda value: value):
        if not self.paired:
            return [lax.all_gather(shard, GROUP, axis=0, tiled=True)]
        two, one = self.two(shard), self.one(shard)
        return [shard, one, two, self.one(wait(two))]

    def share(self, near):
        if not self.paired:
            return near
        return near + [self.inner(piece) for piece in near]

    def parts(self, rows):
        if not self.paired:
            return [(rows, F32)]
        return [(rows // 2, F32), (rows // 2, BF16)]

    def reduce(self, parts, meanwhile):
        if not self.paired:
            total = lax.psum_scatter(parts[0], GROUP, scatter_dimension=0, tiled=True)
            return total.astype(BF16)
        mine, other = parts
        near = mine + meanwhile(None, self.inner(other)).astype(F32)
        shard = near.shape[0] // 4
        own, one, two, both = (near[i * shard : (i + 1) * shard] for i in range(4))
        half = own.shape[1] // 2
        both = both.astype(BF16)
        left = meanwhile(both, self.one(both[:, :half]))
        right = self.two(both[:, half:])
        two = jnp.concatenate([two[:, :half] + left.astype(F32), two[:, half:]], axis=1)
        one = jnp.concatenate([one[:, :half], one[:, half:] + right.astype(F32)], axis=1)
        two, one = two.astype(BF16), one.astype(BF16)
        one = meanwhile(one, self.one(one))
        two = self.two(two)
        return (own + one.astype(F32) + two.astype(F32)).astype(BF16)


def shifted(value, axis, steps):
    count = lax.axis_size(axis)
    pairs = [(source, (source + steps) % count) for source in range(count)]
    return lax.ppermute(value, axis, pairs)


def per_device(
    exchange, tokens, grad_out, w_in, w_down, projector, moment_first, moment_second
):
    units = w_in.shape[2]
    block = block_of(units, 256)
    rows = tokens.shape[1] * exchange.tensor * exchange.dp
    limit = vmem_limit(rows, w_in, exchange)
    early = max(block, block * (units // block // 2))
    held, loaded = load(w_in, early, limit)
    token_rows = exchange.share(exchange.gather(tokens[0], lambda two: after(two, loaded)))
    grad_rows = exchange.gather(grad_out[0])
    hidden, gate_factor, up_factor, mark, held = activations(
        token_rows, w_in, w_down, held, early, limit
    )
    if len(grad_rows) > 1:
        grad_rows = grad_rows[:3] + [after(piece, mark) for piece in grad_rows[3:]]
    grad_rows = exchange.share(grad_rows)
    parts = input_grads(grad_rows, w_down, held, gate_factor, up_factor, exchange, limit)
    cut = max(block, block * (units // block // 3))
    ends = sorted({0, min(cut, units), max(units - cut, 0), units})
    ranges = [(start, end - start) for start, end in zip(ends, ends[1:])]
    moments = moment_first, moment_second
    projector = resident(projector)
    grad_proj, ready = projected(
        grad_rows[:-1] + [after(grad_rows[-1], parts[0])],
        projector,
        *moments,
        sum(count for _, count in ranges[:2]),
    )
    update = None

    def step(value):
        nonlocal update
        start, count = ranges.pop(0)
        update, mark = adam_update(
            hidden, after(grad_proj, value), projector, ready, moments, start, count, update
        )
        return mark

    def meanwhile(sent, received):
        if sent is None:
            return after(received, grad_proj)
        return after(received, step(sent)) if len(ranges) > 1 else received

    total = exchange.reduce(parts, meanwhile)
    passed = shifted(total, "pipe", -1)
    while ranges:
        step(total)
    return (passed[None], update)


def solution(mesh):
    spec = P("pipe", GROUP, None)
    return jax.shard_map(
        functools.partial(per_device, Exchange(mesh)),
        mesh=mesh,
        in_specs=(spec, spec, P("pipe", None, GROUP, None), spec, P("pipe", None, None), spec, spec),
        out_specs=(spec, spec),
        check_vma=False,
    )
```

```python
import functools

import jax
import jax.numpy as jnp
from jax import lax
from jax.experimental import pallas as pl
from jax.experimental.pallas import tpu as pltpu
from jax.sharding import PartitionSpec as P

beta_one = 0.9
beta_two = 0.999
bias_one = 1.0 - 0.9**10
bias_two = 1.0 - 0.999**10
epsilon = 1e-08

BF16 = jnp.bfloat16
F32 = jnp.float32
LANES = 128
MIB = 2**20
VMEM = pl.BlockSpec(memory_space=pltpu.VMEM)
ANY = pl.BlockSpec(memory_space=pl.ANY)
HBM = pl.BlockSpec(memory_space=pltpu.HBM)
GROUP = ("tensor", "dp")


def dot_nn(a, b):
    return jnp.dot(a, b, preferred_element_type=F32)


def dot_nt(a, b):
    return lax.dot_general(a, b, (((1,), (1,)), ((), ())), preferred_element_type=F32)


def block_of(extent, largest):
    sizes = [size for size in range(LANES, largest + 1, LANES) if extent % size == 0]
    return max(sizes, default=extent)


def params(*scratch_bytes):
    return pltpu.CompilerParams(vmem_limit_bytes=max(6 * MIB, MIB + sum(scratch_bytes)))


def resident(value):
    return pltpu.with_memory_space_constraint(value, pltpu.VMEM)


def in_hbm(value):
    return pltpu.with_memory_space_constraint(value, pltpu.HBM)


def cost(flops, *arrays):
    moved = sum(a.size * a.dtype.itemsize for a in arrays)
    return pl.CostEstimate(flops=flops, bytes_accessed=moved, transcendentals=0)


def fill(pieces, rows_ref):
    row = column = 0
    for piece in pieces:
        rows, columns = piece.shape
        rows_ref[row : row + rows, column : column + columns] = piece[...]
        column += columns
        if column == rows_ref.shape[1]:
            row, column = row + rows, 0


def rows_of(pieces, depth):
    return sum(piece.size for piece in pieces) // depth


MARK = jax.ShapeDtypeStruct((8, LANES), F32)


def after_kernel(*_):
    pass


def after(value, *others):
    return pl.pallas_call(
        after_kernel,
        name="after",
        in_specs=[ANY] * (1 + len(others)),
        out_specs=ANY,
        out_shape=jax.ShapeDtypeStruct(value.shape, value.dtype),
        input_output_aliases={0: 0},
        compiler_params=params(),
        cost_estimate=pl.CostEstimate(flops=0, bytes_accessed=0, transcendentals=0),
    )(value, *others)


def stream(reads, slots):
    for read in reads[:slots]:
        read.start()

    def wait(step):
        reads[step].wait()

    def refill(step):
        if step + slots < len(reads):
            reads[step + slots].start()

    return wait, refill


def block_reads(w_ref, held_ref, sems, start, stop):
    units = w_ref.shape[2]
    block = block_of(units, 256)
    return [
        [
            pltpu.make_async_copy(
                w_ref.at[0, which, pl.ds(at, block), :],
                held_ref.at[pl.ds(2 * at + which * block, block), :],
                sems.at[at // block, which],
            )
            for which in range(2)
        ]
        for at in range(start, stop, block)
    ]


def down_early(units):
    block = block_of(units, 256)
    return block * -(-units // (2 * block)) - (block if units > block else 0)


def load_kernel(units, w_ref, held_ref, mark_ref, sems):
    pairs = block_reads(w_ref, held_ref, sems, 0, units)
    for pair in pairs:
        for read in pair:
            read.start()
    mark_ref[...] = jnp.zeros_like(mark_ref)
    for pair in pairs:
        for read in pair:
            read.wait()


def load(w_in, units, limit):
    _, _, all_units, depth = w_in.shape
    return pl.pallas_call(
        functools.partial(load_kernel, units),
        name="load",
        in_specs=[HBM],
        out_specs=[VMEM, VMEM],
        out_shape=[pltpu.VMEM((2 * all_units + down_early(all_units), depth), w_in.dtype), MARK],
        scratch_shapes=[pltpu.SemaphoreType.DMA((units // block_of(all_units, 256), 2))],
        compiler_params=params(limit),
        cost_estimate=cost(0),
    )(in_hbm(w_in))


def act_kernel(count, loaded, *refs):
    pieces, w_ref, down_ref = refs[:count], refs[count], refs[count + 1]
    outs, (rows_ref, sems, down_sem) = refs[count + 3 : -3], refs[-3:]
    hidden_ref, gate_ref, up_ref, mark_ref, held_ref = outs
    _, units, depth = down_ref.shape
    block = block_of(units, 256)
    pairs = block_reads(w_ref, held_ref, sems, loaded, units)
    for pair in pairs:
        for read in pair:
            read.start()
    down_read = pltpu.make_async_copy(
        down_ref.at[0, pl.ds(0, held_ref.shape[0] - 2 * units), :],
        held_ref.at[pl.ds(2 * units, held_ref.shape[0] - 2 * units), :],
        down_sem,
    )
    mark_ref[...] = jnp.zeros_like(mark_ref)
    fill(pieces, rows_ref)

    def finish(at, pre):
        gate_pre, up_act = pre[:, :block], pre[:, block:]
        sigmoid = 1.0 / (1.0 + jnp.exp(-gate_pre))
        silu = gate_pre * sigmoid
        here = slice(at, at + block)
        hidden_ref[here, :] = (silu * up_act).T.astype(BF16)
        gate_ref[:, here] = up_act * sigmoid * (1.0 + gate_pre * (1.0 - sigmoid))
        up_ref[:, here] = silu

    for at in range(0, units, block):
        if at >= loaded:
            for read in pairs[(at - loaded) // block]:
                read.wait()
        pre = dot_nt(rows_ref[...], held_ref[2 * at : 2 * (at + block), :])
        if at == 0:
            down_read.start()
        else:
            finish(at - block, before)
        before = pre
    finish(units - block, before)
    down_read.wait()


def activations(pieces, w_in, w_down, held, loaded, limit):
    _, _, units, depth = w_in.shape
    rows = rows_of(pieces, depth)
    out_shape = [
        jax.ShapeDtypeStruct((units, rows), BF16),
        jax.ShapeDtypeStruct((rows, units), F32),
        jax.ShapeDtypeStruct((rows, units), F32),
        MARK,
        pltpu.VMEM(held.shape, held.dtype),
    ]
    return pl.pallas_call(
        functools.partial(act_kernel, len(pieces), loaded),
        name="activations",
        in_specs=[VMEM] * len(pieces) + [HBM, HBM, VMEM],
        out_specs=[VMEM] * 5,
        out_shape=out_shape,
        input_output_aliases={len(pieces) + 2: 4},
        scratch_shapes=[
            pltpu.VMEM((rows, depth), BF16),
            pltpu.SemaphoreType.DMA((units // block_of(units, 256), 2)),
            pltpu.SemaphoreType.DMA,
        ],
        compiler_params=params(limit),
        cost_estimate=cost(4 * rows * units * depth),
    )(*pieces, in_hbm(w_in), in_hbm(w_down), held)


def input_grad_kernel(count, *refs):
    pieces = refs[:count]
    down_ref, held_ref, gate_ref, up_ref = refs[count : count + 4]
    outs, (rows_ref, grads_ref, slots_ref, sems) = refs[count + 4 : -4], refs[-4:]
    units, depth = gate_ref.shape[1], held_ref.shape[1]
    early = held_ref.shape[0] - 2 * units
    slots, step, _ = slots_ref.shape
    rest = range(early, units, step)
    wait, refill = stream(
        [
            pltpu.make_async_copy(
                down_ref.at[0, pl.ds(start, step), :],
                slots_ref.at[number % slots],
                sems.at[number % slots],
            )
            for number, start in enumerate(rest)
        ],
        slots,
    )
    fill(pieces, rows_ref)

    def factor(start, grad):
        for at in range(start, start + grad.shape[1], step):
            here, part = slice(at, at + step), grad[:, at - start : at - start + step]
            grads_ref[:, 2 * at : 2 * at + step] = (part * gate_ref[:, here]).astype(BF16)
            grads_ref[:, 2 * at + step : 2 * (at + step)] = (part * up_ref[:, here]).astype(BF16)

    wide = min(units, 2 * step)
    for start in range(0, early, wide):
        stop = min(start + wide, early)
        factor(start, dot_nt(rows_ref[...], held_ref[2 * units + start : 2 * units + stop, :]))
    for number, start in enumerate(rest):
        wait(number)
        grad = dot_nt(rows_ref[...], slots_ref[number % slots])
        refill(number)
        factor(start, grad)
    block = block_of(depth, 1024)
    for start in range(0, depth, block):
        here = slice(start, start + block)
        total = dot_nn(grads_ref[...], held_ref[: 2 * units, here])
        row = 0
        for out_ref in outs:
            rows = out_ref.shape[0]
            out_ref[:, here] = total[row : row + rows].astype(out_ref.dtype)
            row += rows


def vmem_limit(rows, w_in, exchange):
    _, _, units, depth = w_in.shape
    work = 8 * rows * max(min(units, 512), block_of(depth, 1024))
    slots = 2 * block_of(units, 256) if units > block_of(units, 256) else 0
    scratch = 2 * rows * depth + 4 * rows * units + 2 * slots * depth
    return scratch + (work if exchange.paired else 3 * work + 4 * rows * depth)


def input_grads(pieces, w_down, held, gate_factor, up_factor, exchange, limit):
    rows, units = gate_factor.shape
    depth = held.shape[1]
    parts = exchange.parts(rows)
    step = block_of(units, 256)
    out_shape = [jax.ShapeDtypeStruct((count, depth), dtype) for count, dtype in parts]
    return pl.pallas_call(
        functools.partial(input_grad_kernel, len(pieces)),
        name="input_grads",
        in_specs=[VMEM] * len(pieces) + [HBM] + [VMEM] * 3,
        out_specs=[VMEM] * len(parts),
        out_shape=out_shape,
        scratch_shapes=[
            pltpu.VMEM((rows, depth), BF16),
            pltpu.VMEM((rows, 2 * units), BF16),
            pltpu.VMEM((2 if units > step else 1, step, depth), BF16),
            pltpu.SemaphoreType.DMA((2 if units > step else 1,)),
        ],
        compiler_params=params(limit),
        cost_estimate=cost(6 * rows * units * depth, *out_shape),
    )(*pieces, in_hbm(w_down), held, gate_factor, up_factor)


def project_kernel(count, *refs):
    pieces = refs[:count]
    proj_ref, first_ref, second_ref, out_ref, moments_ref, rows_ref, sems = refs[count:]
    here = pl.ds(0, moments_ref.shape[1])
    reads = [
        pltpu.make_async_copy(ref.at[0, here, :], moments_ref.at[which], sems.at[which])
        for which, ref in enumerate((first_ref, second_ref))
    ]
    for read in reads:
        read.start()
    fill(pieces, rows_ref)
    out_ref[...] = dot_nn(rows_ref[...], proj_ref[0]).astype(BF16)
    for read in reads:
        read.wait()


def projected(pieces, projector, moment_first, moment_second, units):
    _, depth, rank = projector.shape
    rows = rows_of(pieces, depth)
    out_shape = [
        jax.ShapeDtypeStruct((rows, rank), BF16),
        pltpu.VMEM((2, units, rank), F32),
    ]
    return pl.pallas_call(
        functools.partial(project_kernel, len(pieces)),
        name="projected",
        in_specs=[VMEM] * (len(pieces) + 1) + [HBM] * 2,
        out_specs=[VMEM] * 2,
        out_shape=out_shape,
        scratch_shapes=[pltpu.VMEM((rows, depth), BF16), pltpu.SemaphoreType.DMA((2,))],
        compiler_params=adam_params(depth, rank, rows),
        cost_estimate=cost(2 * rows * depth * rank, projector),
    )(*pieces, projector, in_hbm(moment_first), in_hbm(moment_second))


def adam_params(depth, rank, rows):
    return params(2 * rows * depth, 8 * rows * rank, 20 * 2**20)


def adam_kernel(start, block, held, ready, *refs):
    hidden_ref, grad_proj_ref, proj_ref, ready_ref, first_ref, second_ref = refs[:6]
    out_ref, mark_ref, normed_ref, moments_ref, slots_ref, in_sems, out_sems = refs[6 + held :]
    units, depth = normed_ref.shape[0], proj_ref.shape[1]
    width = block_of(depth, 1024)
    steps = range(0, units, block)

    reads = []
    for step, at in enumerate(() if ready else steps):
        there = pl.ds(start + at, block)
        for which, ref in enumerate((first_ref, second_ref)):
            reads.append(
                pltpu.make_async_copy(
                    ref.at[0, there, :],
                    moments_ref.at[which, pl.ds(at, block), :],
                    in_sems.at[which, step],
                )
            )
    for read in reads:
        read.start()
    mark_ref[...] = jnp.zeros_like(mark_ref)

    def wait(step):
        for read in reads[2 * step : 2 * step + 2]:
            read.wait()

    def moments(which, here):
        if ready:
            return ready_ref[which, start + here.start : start + here.stop, :]
        return moments_ref[which, here, :]

    def normalise(step):
        here = slice(step * block, (step + 1) * block)
        low_grad = dot_nn(
            hidden_ref[start + here.start : start + here.stop, :], grad_proj_ref[...]
        )
        first = beta_one * moments(0, here) + (1.0 - beta_one) * low_grad
        second = beta_two * moments(1, here) + (1.0 - beta_two) * low_grad * low_grad
        normed = first / bias_one / (jnp.sqrt(second / bias_two) + epsilon)
        normed_ref[here, :] = normed.astype(BF16)

    writes = []
    wait(0)
    normalise(0)
    for step, at in enumerate(steps):
        slot = step % 2
        if step >= 2:
            for write in writes[step - 2]:
                write.wait()
        if step + 1 < len(steps):
            wait(step + 1)
            normalise(step + 1)
        for column in range(0, depth, width):
            here = slice(column, column + width)
            back = dot_nt(normed_ref[at : at + block, :], proj_ref[0, here, :])
            slots_ref[slot, :, here] = back.astype(BF16)
            write = pltpu.make_async_copy(
                slots_ref.at[slot, :, pl.ds(column, width)],
                out_ref.at[0, pl.ds(start + at, block), pl.ds(column, width)],
                out_sems.at[slot, column // width],
            )
            write.start()
            if not column:
                writes.append([])
            writes[-1].append(write)
    for step in writes[-2:]:
        for write in step:
            write.wait()


def adam_update(hidden, grad_proj, projector, ready, moments, start, units, out=None):
    rows = hidden.shape[1]
    _, all_units, rank = moments[0].shape
    depth = projector.shape[1]
    block = block_of(all_units, 256)
    held = [] if out is None else [out]
    early = start + units <= ready.shape[1]
    out_shape = jax.ShapeDtypeStruct((1, all_units, depth), BF16)
    return pl.pallas_call(
        functools.partial(adam_kernel, start, block, len(held), early),
        name="adam_update",
        in_specs=[VMEM] * 4 + [HBM] * (2 + len(held)),
        out_specs=[HBM, VMEM],
        out_shape=[out_shape, MARK],
        input_output_aliases={6: 0} if held else {},
        scratch_shapes=[
            pltpu.VMEM((units, rank), BF16),
            pltpu.VMEM((2, block if early else units, rank), F32),
            pltpu.VMEM((2, block, depth), BF16),
            pltpu.SemaphoreType.DMA((2, units // block)),
            pltpu.SemaphoreType.DMA((2, depth // block_of(depth, 1024))),
        ],
        compiler_params=adam_params(depth, rank, rows),
        cost_estimate=pl.CostEstimate(
            flops=2 * units * rank * (rows + depth), bytes_accessed=2 * units * depth, transcendentals=0
        ),
    )(hidden, grad_proj, projector, ready, *map(in_hbm, moments), *held)


class Exchange:
    def __init__(self, mesh):
        self.tensor, self.dp = mesh.shape["tensor"], mesh.shape["dp"]
        self.paired = self.tensor == 2 and self.dp == 4

    def swap(self, value, partner):
        pairs = []
        for t in range(self.tensor):
            for d in range(self.dp):
                to_t, to_d = partner(t, d)
                pairs.append((t * self.dp + d, to_t * self.dp + to_d))
        return lax.ppermute(value, GROUP, pairs)

    def inner(self, value):
        return self.swap(value, lambda t, d: (t, d ^ 1))

    def one(self, value):
        return self.swap(value, lambda t, d: (t ^ (d & 1), d ^ (0 if d & 1 else 2)))

    def two(self, value):
        return self.swap(value, lambda t, d: (t ^ (1 - (d & 1)), d ^ (2 if d & 1 else 0)))

    def gather(self, shard, wait=lambda value: value, halves=False):
        if not self.paired:
            return [lax.all_gather(shard, GROUP, axis=0, tiled=True)]
        two, one = self.two(shard), self.one(shard)
        if not halves:
            return [shard, one, two, self.one(wait(two))]
        half = shard.shape[1] // 2
        two = wait(two)
        return [shard, one, two, self.one(two[:, :half]), self.two(one[:, half:])]

    def share(self, near):
        if not self.paired:
            return near
        return near + [self.inner(piece) for piece in near]

    def parts(self, rows):
        if not self.paired:
            return [(rows, F32)]
        return [(rows // 2, F32), (rows // 2, BF16)]

    def reduce(self, parts, meanwhile):
        if not self.paired:
            total = lax.psum_scatter(parts[0], GROUP, scatter_dimension=0, tiled=True)
            return total.astype(BF16)
        mine, other = parts
        near = mine + meanwhile(None, self.inner(other)).astype(F32)
        shard = near.shape[0] // 4
        own, one, two, both = (near[i * shard : (i + 1) * shard] for i in range(4))
        half = own.shape[1] // 2
        both = both.astype(BF16)
        left = meanwhile(both, self.one(both[:, :half]))
        right = self.two(both[:, half:])
        two = jnp.concatenate([two[:, :half] + left.astype(F32), two[:, half:]], axis=1)
        one = jnp.concatenate([one[:, :half], one[:, half:] + right.astype(F32)], axis=1)
        two, one = two.astype(BF16), one.astype(BF16)
        one = meanwhile(one, self.one(one))
        two = self.two(two)
        return (own + one.astype(F32) + two.astype(F32)).astype(BF16)


def shifted(value, axis, steps):
    count = lax.axis_size(axis)
    pairs = [(source, (source + steps) % count) for source in range(count)]
    return lax.ppermute(value, axis, pairs)


def per_device(
    exchange, tokens, grad_out, w_in, w_down, projector, moment_first, moment_second
):
    units = w_in.shape[2]
    block = block_of(units, 256)
    rows = tokens.shape[1] * exchange.tensor * exchange.dp
    limit = vmem_limit(rows, w_in, exchange)
    early = max(block, block * (units // block // 2))
    held, loaded = load(w_in, early, limit)
    token_rows = exchange.share(exchange.gather(tokens[0], lambda two: after(two, loaded), True))
    grad_rows = exchange.gather(grad_out[0])
    hidden, gate_factor, up_factor, mark, held = activations(
        token_rows, w_in, w_down, held, early, limit
    )
    if len(grad_rows) > 1:
        own, one, two, *both = grad_rows
        grad_rows = [own, after(one, mark), two] + [after(piece, mark) for piece in both]
    grad_rows = exchange.share(grad_rows)
    parts = input_grads(grad_rows, w_down, held, gate_factor, up_factor, exchange, limit)
    cut = max(block, block * (units // block // 3))
    ends = sorted({0, min(cut, units), max(units - cut, 0), units})
    ranges = [(start, end - start) for start, end in zip(ends, ends[1:])]
    moments = moment_first, moment_second
    projector = resident(projector)
    grad_proj, ready = projected(
        grad_rows[:-1] + [after(grad_rows[-1], parts[0])],
        projector,
        *moments,
        sum(count for _, count in ranges[:2]),
    )
    update = None

    def step(value):
        nonlocal update
        start, count = ranges.pop(0)
        update, mark = adam_update(
            hidden, after(grad_proj, value), projector, ready, moments, start, count, update
        )
        return mark

    def meanwhile(sent, received):
        if sent is None:
            return after(received, grad_proj)
        return after(received, step(sent)) if len(ranges) > 1 else received

    total = exchange.reduce(parts, meanwhile)
    passed = shifted(total, "pipe", -1)
    while ranges:
        step(total)
    return (passed[None], update)


def solution(mesh):
    spec = P("pipe", GROUP, None)
    return jax.shard_map(
        functools.partial(per_device, Exchange(mesh)),
        mesh=mesh,
        in_specs=(spec, spec, P("pipe", None, GROUP, None), spec, P("pipe", None, None), spec, spec),
        out_specs=(spec, spec),
        check_vma=False,
    )
```

```python
import functools

import jax
import jax.numpy as jnp
from jax import lax
from jax.experimental import pallas as pl
from jax.experimental.pallas import tpu as pltpu
from jax.sharding import PartitionSpec as P

beta_one = 0.9
beta_two = 0.999
bias_one = 1.0 - 0.9**10
bias_two = 1.0 - 0.999**10
epsilon = 1e-08

BF16 = jnp.bfloat16
F32 = jnp.float32
LANES = 128
MIB = 2**20
VMEM = pl.BlockSpec(memory_space=pltpu.VMEM)
ANY = pl.BlockSpec(memory_space=pl.ANY)
HBM = pl.BlockSpec(memory_space=pltpu.HBM)
GROUP = ("tensor", "dp")


def dot_nn(a, b):
    return jnp.dot(a, b, preferred_element_type=F32)


def dot_nt(a, b):
    return lax.dot_general(a, b, (((1,), (1,)), ((), ())), preferred_element_type=F32)


def block_of(extent, largest):
    sizes = [size for size in range(LANES, largest + 1, LANES) if extent % size == 0]
    return max(sizes, default=extent)


def params(*scratch_bytes):
    return pltpu.CompilerParams(vmem_limit_bytes=max(6 * MIB, MIB + sum(scratch_bytes)))


def resident(value):
    return pltpu.with_memory_space_constraint(value, pltpu.VMEM)


def in_hbm(value):
    return pltpu.with_memory_space_constraint(value, pltpu.HBM)


def cost(flops, *arrays):
    moved = sum(a.size * a.dtype.itemsize for a in arrays)
    return pl.CostEstimate(flops=flops, bytes_accessed=moved, transcendentals=0)


def fill(pieces, rows_ref):
    row = column = 0
    for piece in pieces:
        rows, columns = piece.shape
        rows_ref[row : row + rows, column : column + columns] = piece[...]
        column += columns
        if column == rows_ref.shape[1]:
            row, column = row + rows, 0


def rows_of(pieces, depth):
    return sum(piece.size for piece in pieces) // depth


MARK = jax.ShapeDtypeStruct((8, LANES), F32)


def after_kernel(*_):
    pass


def after(value, *others):
    return pl.pallas_call(
        after_kernel,
        name="after",
        in_specs=[ANY] * (1 + len(others)),
        out_specs=ANY,
        out_shape=jax.ShapeDtypeStruct(value.shape, value.dtype),
        input_output_aliases={0: 0},
        compiler_params=params(),
        cost_estimate=pl.CostEstimate(flops=0, bytes_accessed=0, transcendentals=0),
    )(value, *others)


def stream(reads, slots):
    for read in reads[:slots]:
        read.start()

    def wait(step):
        reads[step].wait()

    def refill(step):
        if step + slots < len(reads):
            reads[step + slots].start()

    return wait, refill


def block_reads(w_ref, held_ref, sems, start, stop):
    units = w_ref.shape[2]
    block = block_of(units, 256)
    return [
        [
            pltpu.make_async_copy(
                w_ref.at[0, which, pl.ds(at, block), :],
                held_ref.at[pl.ds(2 * at + which * block, block), :],
                sems.at[at // block, which],
            )
            for which in range(2)
        ]
        for at in range(start, stop, block)
    ]


def down_early(units):
    block = block_of(units, 256)
    return block * -(-units // (2 * block)) - (block if units > block else 0)


def load_kernel(units, w_ref, held_ref, mark_ref, sems):
    pairs = block_reads(w_ref, held_ref, sems, 0, units)
    for pair in pairs:
        for read in pair:
            read.start()
    mark_ref[...] = jnp.zeros_like(mark_ref)
    for pair in pairs:
        for read in pair:
            read.wait()


def load(w_in, units, limit):
    _, _, all_units, depth = w_in.shape
    return pl.pallas_call(
        functools.partial(load_kernel, units),
        name="load",
        in_specs=[HBM],
        out_specs=[VMEM, VMEM],
        out_shape=[pltpu.VMEM((2 * all_units + down_early(all_units), depth), w_in.dtype), MARK],
        scratch_shapes=[pltpu.SemaphoreType.DMA((units // block_of(all_units, 256), 2))],
        compiler_params=params(limit),
        cost_estimate=cost(0),
    )(in_hbm(w_in))


def act_kernel(count, loaded, *refs):
    pieces, w_ref, down_ref = refs[:count], refs[count], refs[count + 1]
    outs, (rows_ref, sems, down_sem) = refs[count + 3 : -3], refs[-3:]
    hidden_ref, gate_ref, up_ref, mark_ref, held_ref = outs
    _, units, depth = down_ref.shape
    block = block_of(units, 256)
    pairs = block_reads(w_ref, held_ref, sems, loaded, units)
    for pair in pairs:
        for read in pair:
            read.start()
    down_read = pltpu.make_async_copy(
        down_ref.at[0, pl.ds(0, held_ref.shape[0] - 2 * units), :],
        held_ref.at[pl.ds(2 * units, held_ref.shape[0] - 2 * units), :],
        down_sem,
    )
    mark_ref[...] = jnp.zeros_like(mark_ref)
    fill(pieces, rows_ref)

    def finish(at, pre):
        gate_pre, up_act = pre[:, :block], pre[:, block:]
        sigmoid = 1.0 / (1.0 + jnp.exp(-gate_pre))
        silu = gate_pre * sigmoid
        here = slice(at, at + block)
        hidden_ref[here, :] = (silu * up_act).T.astype(BF16)
        gate_ref[:, here] = up_act * sigmoid * (1.0 + gate_pre * (1.0 - sigmoid))
        up_ref[:, here] = silu

    for at in range(0, units, block):
        if at >= loaded:
            for read in pairs[(at - loaded) // block]:
                read.wait()
        pre = dot_nt(rows_ref[...], held_ref[2 * at : 2 * (at + block), :])
        if at == 0:
            down_read.start()
        else:
            finish(at - block, before)
        before = pre
    finish(units - block, before)
    down_read.wait()


def activations(pieces, w_in, w_down, held, loaded, limit):
    _, _, units, depth = w_in.shape
    rows = rows_of(pieces, depth)
    out_shape = [
        jax.ShapeDtypeStruct((units, rows), BF16),
        jax.ShapeDtypeStruct((rows, units), F32),
        jax.ShapeDtypeStruct((rows, units), F32),
        MARK,
        pltpu.VMEM(held.shape, held.dtype),
    ]
    return pl.pallas_call(
        functools.partial(act_kernel, len(pieces), loaded),
        name="activations",
        in_specs=[VMEM] * len(pieces) + [HBM, HBM, VMEM],
        out_specs=[VMEM] * 5,
        out_shape=out_shape,
        input_output_aliases={len(pieces) + 2: 4},
        scratch_shapes=[
            pltpu.VMEM((rows, depth), BF16),
            pltpu.SemaphoreType.DMA((units // block_of(units, 256), 2)),
            pltpu.SemaphoreType.DMA,
        ],
        compiler_params=params(limit),
        cost_estimate=cost(4 * rows * units * depth),
    )(*pieces, in_hbm(w_in), in_hbm(w_down), held)


def input_grad_kernel(count, *refs):
    pieces = refs[:count]
    down_ref, held_ref, gate_ref, up_ref = refs[count : count + 4]
    outs, (rows_ref, grads_ref, slots_ref, sems) = refs[count + 4 : -4], refs[-4:]
    units, depth = gate_ref.shape[1], held_ref.shape[1]
    early = held_ref.shape[0] - 2 * units
    slots, step, _ = slots_ref.shape
    rest = range(early, units, step)
    wait, refill = stream(
        [
            pltpu.make_async_copy(
                down_ref.at[0, pl.ds(start, step), :],
                slots_ref.at[number % slots],
                sems.at[number % slots],
            )
            for number, start in enumerate(rest)
        ],
        slots,
    )
    fill(pieces, rows_ref)

    def factor(start, grad):
        for at in range(start, start + grad.shape[1], step):
            here, part = slice(at, at + step), grad[:, at - start : at - start + step]
            grads_ref[:, 2 * at : 2 * at + step] = (part * gate_ref[:, here]).astype(BF16)
            grads_ref[:, 2 * at + step : 2 * (at + step)] = (part * up_ref[:, here]).astype(BF16)

    wide = min(units, 2 * step)
    for start in range(0, early, wide):
        stop = min(start + wide, early)
        factor(start, dot_nt(rows_ref[...], held_ref[2 * units + start : 2 * units + stop, :]))
    for number, start in enumerate(rest):
        wait(number)
        grad = dot_nt(rows_ref[...], slots_ref[number % slots])
        refill(number)
        factor(start, grad)
    block = block_of(depth, 1024)
    for start in range(0, depth, block):
        here = slice(start, start + block)
        total = dot_nn(grads_ref[...], held_ref[: 2 * units, here])
        row = 0
        for out_ref in outs:
            rows = out_ref.shape[0]
            out_ref[:, here] = total[row : row + rows].astype(out_ref.dtype)
            row += rows


def vmem_limit(rows, w_in, exchange):
    _, _, units, depth = w_in.shape
    work = 8 * rows * max(min(units, 512), block_of(depth, 1024))
    slots = 2 * block_of(units, 256) if units > block_of(units, 256) else 0
    scratch = 2 * rows * depth + 4 * rows * units + 2 * slots * depth
    return scratch + (work if exchange.paired else 3 * work + 4 * rows * depth)


def input_grads(pieces, w_down, held, gate_factor, up_factor, exchange, limit):
    rows, units = gate_factor.shape
    depth = held.shape[1]
    parts = exchange.parts(rows)
    step = block_of(units, 256)
    out_shape = [jax.ShapeDtypeStruct((count, depth), dtype) for count, dtype in parts]
    return pl.pallas_call(
        functools.partial(input_grad_kernel, len(pieces)),
        name="input_grads",
        in_specs=[VMEM] * len(pieces) + [HBM] + [VMEM] * 3,
        out_specs=[VMEM] * len(parts),
        out_shape=out_shape,
        scratch_shapes=[
            pltpu.VMEM((rows, depth), BF16),
            pltpu.VMEM((rows, 2 * units), BF16),
            pltpu.VMEM((2 if units > step else 1, step, depth), BF16),
            pltpu.SemaphoreType.DMA((2 if units > step else 1,)),
        ],
        compiler_params=params(limit),
        cost_estimate=cost(6 * rows * units * depth, *out_shape),
    )(*pieces, in_hbm(w_down), held, gate_factor, up_factor)


def project_kernel(count, *refs):
    pieces = refs[:count]
    proj_ref, first_ref, second_ref, out_ref, moments_ref, rows_ref, sems = refs[count:]
    here = pl.ds(0, moments_ref.shape[1])
    reads = [
        pltpu.make_async_copy(ref.at[0, here, :], moments_ref.at[which], sems.at[which])
        for which, ref in enumerate((first_ref, second_ref))
    ]
    for read in reads:
        read.start()
    fill(pieces, rows_ref)
    out_ref[...] = dot_nn(rows_ref[...], proj_ref[0]).astype(BF16)
    for read in reads:
        read.wait()


def projected(pieces, projector, moment_first, moment_second, units):
    _, depth, rank = projector.shape
    rows = rows_of(pieces, depth)
    out_shape = [
        jax.ShapeDtypeStruct((rows, rank), BF16),
        pltpu.VMEM((2, units, rank), F32),
    ]
    return pl.pallas_call(
        functools.partial(project_kernel, len(pieces)),
        name="projected",
        in_specs=[VMEM] * (len(pieces) + 1) + [HBM] * 2,
        out_specs=[VMEM] * 2,
        out_shape=out_shape,
        scratch_shapes=[pltpu.VMEM((rows, depth), BF16), pltpu.SemaphoreType.DMA((2,))],
        compiler_params=adam_params(depth, rank, rows),
        cost_estimate=cost(2 * rows * depth * rank, projector),
    )(*pieces, projector, in_hbm(moment_first), in_hbm(moment_second))


def adam_params(depth, rank, rows):
    return params(2 * rows * depth, 8 * rows * rank, 20 * 2**20)


def adam_kernel(start, block, held, ready, *refs):
    hidden_ref, grad_proj_ref, proj_ref, ready_ref, first_ref, second_ref = refs[:6]
    out_ref, mark_ref, normed_ref, moments_ref, slots_ref, in_sems, out_sems = refs[6 + held :]
    units, depth = normed_ref.shape[0], proj_ref.shape[1]
    width = block_of(depth, 1024)
    steps = range(0, units, block)

    reads = []
    for step, at in enumerate(() if ready else steps):
        there = pl.ds(start + at, block)
        for which, ref in enumerate((first_ref, second_ref)):
            reads.append(
                pltpu.make_async_copy(
                    ref.at[0, there, :],
                    moments_ref.at[which, pl.ds(at, block), :],
                    in_sems.at[which, step],
                )
            )
    for read in reads:
        read.start()
    mark_ref[...] = jnp.zeros_like(mark_ref)

    def wait(step):
        for read in reads[2 * step : 2 * step + 2]:
            read.wait()

    def moments(which, here):
        if ready:
            return ready_ref[which, start + here.start : start + here.stop, :]
        return moments_ref[which, here, :]

    def normalise(step):
        here = slice(step * block, (step + 1) * block)
        low_grad = dot_nn(
            hidden_ref[start + here.start : start + here.stop, :], grad_proj_ref[...]
        )
        first = beta_one * moments(0, here) + (1.0 - beta_one) * low_grad
        second = beta_two * moments(1, here) + (1.0 - beta_two) * low_grad * low_grad
        normed = first / bias_one / (jnp.sqrt(second / bias_two) + epsilon)
        normed_ref[here, :] = normed.astype(BF16)

    writes = []
    wait(0)
    normalise(0)
    for step, at in enumerate(steps):
        slot = step % 2
        if step >= 2:
            for write in writes[step - 2]:
                write.wait()
        if step + 1 < len(steps):
            wait(step + 1)
            normalise(step + 1)
        for column in range(0, depth, width):
            here = slice(column, column + width)
            back = dot_nt(normed_ref[at : at + block, :], proj_ref[0, here, :])
            slots_ref[slot, :, here] = back.astype(BF16)
            write = pltpu.make_async_copy(
                slots_ref.at[slot, :, pl.ds(column, width)],
                out_ref.at[0, pl.ds(start + at, block), pl.ds(column, width)],
                out_sems.at[slot, column // width],
            )
            write.start()
            if not column:
                writes.append([])
            writes[-1].append(write)
    for step in writes[-2:]:
        for write in step:
            write.wait()


def adam_update(hidden, grad_proj, projector, ready, moments, start, units, out=None):
    rows = hidden.shape[1]
    _, all_units, rank = moments[0].shape
    depth = projector.shape[1]
    block = block_of(all_units, 256)
    held = [] if out is None else [out]
    early = start + units <= ready.shape[1]
    out_shape = jax.ShapeDtypeStruct((1, all_units, depth), BF16)
    return pl.pallas_call(
        functools.partial(adam_kernel, start, block, len(held), early),
        name="adam_update",
        in_specs=[VMEM] * 4 + [HBM] * (2 + len(held)),
        out_specs=[HBM, VMEM],
        out_shape=[out_shape, MARK],
        input_output_aliases={6: 0} if held else {},
        scratch_shapes=[
            pltpu.VMEM((units, rank), BF16),
            pltpu.VMEM((2, block if early else units, rank), F32),
            pltpu.VMEM((2, block, depth), BF16),
            pltpu.SemaphoreType.DMA((2, units // block)),
            pltpu.SemaphoreType.DMA((2, depth // block_of(depth, 1024))),
        ],
        compiler_params=adam_params(depth, rank, rows),
        cost_estimate=pl.CostEstimate(
            flops=2 * units * rank * (rows + depth), bytes_accessed=2 * units * depth, transcendentals=0
        ),
    )(hidden, grad_proj, projector, ready, *map(in_hbm, moments), *held)


class Exchange:
    def __init__(self, mesh):
        self.tensor, self.dp = mesh.shape["tensor"], mesh.shape["dp"]
        self.paired = self.tensor == 2 and self.dp == 4

    def swap(self, value, partner):
        pairs = []
        for t in range(self.tensor):
            for d in range(self.dp):
                to_t, to_d = partner(t, d)
                pairs.append((t * self.dp + d, to_t * self.dp + to_d))
        return lax.ppermute(value, GROUP, pairs)

    def inner(self, value):
        return self.swap(value, lambda t, d: (t, d ^ 1))

    def one(self, value):
        return self.swap(value, lambda t, d: (t ^ (d & 1), d ^ (0 if d & 1 else 2)))

    def two(self, value):
        return self.swap(value, lambda t, d: (t ^ (1 - (d & 1)), d ^ (2 if d & 1 else 0)))

    def gather(self, shard, wait=lambda value: value, halves=False):
        if not self.paired:
            return [lax.all_gather(shard, GROUP, axis=0, tiled=True)]
        two, one = self.two(shard), self.one(shard)
        if not halves:
            return [shard, one, two, self.one(wait(two))]
        half = shard.shape[1] // 2
        two = wait(two)
        return [shard, one, two, self.one(two[:, :half]), self.two(one[:, half:])]

    def share(self, near):
        if not self.paired:
            return near
        return near + [self.inner(piece) for piece in near]

    def parts(self, rows):
        if not self.paired:
            return [(rows, F32)]
        return [(rows // 2, F32), (rows // 2, BF16)]

    def reduce(self, parts, meanwhile):
        if not self.paired:
            total = lax.psum_scatter(parts[0], GROUP, scatter_dimension=0, tiled=True)
            return total.astype(BF16)
        mine, other = parts
        near = mine + meanwhile(None, self.inner(other)).astype(F32)
        shard = near.shape[0] // 4
        own, one, two, both = (near[i * shard : (i + 1) * shard] for i in range(4))
        half = own.shape[1] // 2
        both = both.astype(BF16)
        left = meanwhile(both, self.one(both[:, :half]))
        right = self.two(both[:, half:])
        two = jnp.concatenate([two[:, :half] + left.astype(F32), two[:, half:]], axis=1)
        one = jnp.concatenate([one[:, :half], one[:, half:] + right.astype(F32)], axis=1)
        two, one = two.astype(BF16), one.astype(BF16)
        one = meanwhile(one, self.one(one))
        two = self.two(two)
        return (own + one.astype(F32) + two.astype(F32)).astype(BF16)


def shifted(value, axis, steps):
    count = lax.axis_size(axis)
    pairs = [(source, (source + steps) % count) for source in range(count)]
    return lax.ppermute(value, axis, pairs)


def per_device(
    exchange, tokens, grad_out, w_in, w_down, projector, moment_first, moment_second
):
    units = w_in.shape[2]
    block = block_of(units, 256)
    rows = tokens.shape[1] * exchange.tensor * exchange.dp
    limit = vmem_limit(rows, w_in, exchange)
    early = max(block, block * (units // block // 2))
    held, loaded = load(w_in, early, limit)
    token_rows = exchange.share(exchange.gather(tokens[0], lambda two: after(two, loaded), True))
    grad_rows = exchange.gather(grad_out[0])
    hidden, gate_factor, up_factor, mark, held = activations(
        token_rows, w_in, w_down, held, early, limit
    )
    if len(grad_rows) > 1:
        own, one, two, *both = grad_rows
        grad_rows = [own, after(one, mark), two] + [after(piece, mark) for piece in both]
    grad_rows = exchange.share(grad_rows)
    parts = input_grads(grad_rows, w_down, held, gate_factor, up_factor, exchange, limit)
    cut = max(block, block * (units // block // 3))
    ends = sorted({0, min(cut, units), min(2 * cut, units), units})
    ranges = [(start, end - start) for start, end in zip(ends, ends[1:])]
    ranges = ranges[:1] + ranges[:0:-1]
    moments = moment_first, moment_second
    projector = resident(projector)
    grad_proj, ready = projected(
        grad_rows[:-1] + [after(grad_rows[-1], parts[0])],
        projector,
        *moments,
        min(2 * cut, units),
    )
    update = None

    def step(value):
        nonlocal update
        start, count = ranges.pop(0)
        update, mark = adam_update(
            hidden, after(grad_proj, value), projector, ready, moments, start, count, update
        )
        return mark

    def meanwhile(sent, received):
        if sent is None:
            return after(received, grad_proj)
        return after(received, step(sent)) if len(ranges) > 1 else received

    total = exchange.reduce(parts, meanwhile)
    passed = shifted(total, "pipe", -1)
    while ranges:
        step(total)
    return (passed[None], update)


def solution(mesh):
    spec = P("pipe", GROUP, None)
    return jax.shard_map(
        functools.partial(per_device, Exchange(mesh)),
        mesh=mesh,
        in_specs=(spec, spec, P("pipe", None, GROUP, None), spec, P("pipe", None, None), spec, spec),
        out_specs=(spec, spec),
        check_vma=False,
    )
```
